32 devices in a mesh: scen: 8 (over z, core), tile: 4 (over y, x).
Axes of the slice: x: 2, y: 2, z: 4, core: 2. Of those that a mesh axis runs over, the one named last changes fastest.
Arguments:
- inv_factor: bfloat16 [32, 1024, 1024], P(('scen', 'tile'))
- border: bfloat16 [32, 1024, 512], P(('scen', 'tile')), may hold values from -0.1875 to 0.1875
- touched: int32 [32, 4], P(('scen', 'tile')), may hold values from 0 to 127, as said below
- live_count: int32 [32], P(('scen', 'tile')), may hold values from 1 to 4, as said below
- regular: float32 [16384], P('scen'), may hold values from 0.5 to 2
Outputs:
- schur_full: float32 [16384, 16384], P('scen', 'tile')
- panel: float32 [16384, 1024], P(('scen', 'tile'))
The draws below stay inside these ranges and needn't reach their ends.
Inputs may be any that keep to these rules, and one draw needn't show every extreme that they name: `touched`: the 4 block numbers of one scenario lie in 4 different groups of 32 consecutive block numbers. Slots 0 to live_count - 1 of a scenario are live; some scenario has all 4 slots live.
All inputs are finite; a program needn't handle non-finite values.
Results may differ from the reference program's by a relative error of at most 0.0012.
Values sent between devices are 32-bit elements; how exact they have to be, the bound alone decides.
No kernel may reach another device: no remote copies, remote signals or barrier semaphores. Data moves between devices by JAX's collectives and lax.ppermute only.
A program may use at most 192 MiB of HBM per device.

```python
import math
import jax
import jax.numpy as jnp
from jax import lax

FIRST = 16384
BLOCK = 128
ORDER = 1024
PANEL = 1024
SLOTS = 4
NBLK = 128
SCENS = 32


def draw_inv_factor(key, part):
    first_key = jax.random.fold_in(key, 101)
    second_key = jax.random.fold_in(key, 102)
    lower_part = jax.random.normal(first_key, (SCENS, ORDER, ORDER), jnp.float32) * ORDER ** (-0.5)
    diagonal = jax.random.uniform(second_key, (SCENS, ORDER), jnp.float32, 0.6, 1.4)
    rows = jnp.arange(ORDER)[:, None]
    cols = jnp.arange(ORDER)[None, :]
    strict = jnp.where(rows > cols, 1.0, 0.0).astype(jnp.float32)
    unit = jnp.where(rows == cols, 1.0, 0.0).astype(jnp.float32)
    whole = lower_part * strict[None, :, :] + diagonal[:, :, None] * unit[None, :, :]
    return whole.astype(jnp.bfloat16)


def draw_touched(key, part):
    group_size = NBLK // SLOTS
    scen_keys = jax.random.split(jax.random.fold_in(key, 201), SCENS)
    groups = jax.vmap(lambda one_key: jax.random.permutation(one_key, SLOTS))(scen_keys)
    offsets = jax.random.randint(jax.random.fold_in(key, 202), (SCENS, SLOTS), 0, group_size)
    return (groups * group_size + offsets).astype(jnp.int32)


def draw_live_count(key, part):
    lowest = max(1, SLOTS // 4)
    counts = jax.random.randint(jax.random.fold_in(key, 301), (SCENS,), lowest, SLOTS + 1)
    chosen = jax.random.randint(jax.random.fold_in(key, 302), (), 0, SCENS)
    counts = jnp.where(jnp.arange(SCENS) == chosen, SLOTS, counts)
    return counts.astype(jnp.int32)


def block_scale(stream_key, shape, pieces, least, largest):
    factor_of, own = 1.0, jax.random.fold_in(stream_key, 6)
    for dim, shards_of in pieces:
        heights = jnp.exp(jax.random.uniform(jax.random.fold_in(own, dim), (shards_of,), jnp.float32, least / len(pieces), largest / len(pieces)))
        factor_of = factor_of * jnp.repeat(heights, shape[dim] // shards_of).reshape([-1 if axis == dim else 1 for axis in range(len(shape))])
    return factor_of


def gaussian(stream_key, shape, spread, reach, pieces=(), held_as=jnp.bfloat16):
    drawn = jax.random.normal(stream_key, shape, jnp.float32) * spread
    if len(pieces) > 0:
        drawn = block_scale(stream_key, shape, pieces, -0.22, 0.18) * drawn
    return jnp.clip(drawn, min=-reach, max=reach).astype(held_as)


def setup_inputs(seed: int = 0) -> dict:
    key_list = jax.random.split(jax.random.key(seed), 6)
    return {
        "inv_factor": draw_inv_factor(jax.random.fold_in(key_list[5], 71), 0),
        "border": gaussian(key_list[1], (SCENS, ORDER, SLOTS * BLOCK), ORDER ** -0.5, 0.1875, ((0, 32),)),
        "touched": draw_touched(jax.random.fold_in(key_list[5], 71), 0),
        "live_count": draw_live_count(jax.random.fold_in(key_list[5], 71), 0),
        "regular": jnp.clip(jnp.exp(math.log(2.0) - 1.3862944 * jax.random.uniform(key_list[4], (FIRST,), jnp.float32) ** block_scale(key_list[4], (FIRST,), ((0, 8),), -0.2, 0.2)), 0.5, 2.0),
    }


def add_scenario(schur_full, scenario):
    inv_block, border_block, block_ids, count = scenario
    scaled = jnp.dot(inv_block.astype(jnp.float32), border_block.astype(jnp.float32), preferred_element_type=jnp.float32).astype(jnp.bfloat16)
    live_mask = (jnp.arange(SLOTS, dtype=jnp.int32) < count).astype(jnp.bfloat16)
    column_mask = jnp.repeat(live_mask, BLOCK)
    scaled = scaled * column_mask[None, :]
    gram_block = jnp.dot(scaled.T.astype(jnp.float32), scaled.astype(jnp.float32), preferred_element_type=jnp.float32)
    indices = (block_ids.astype(jnp.int32)[:, None] * BLOCK + jnp.arange(BLOCK, dtype=jnp.int32)[None, :]).reshape(-1).astype(jnp.int32)
    return (schur_full.at[indices[:, None], indices[None, :]].add(gram_block.astype(schur_full.dtype)), None)

def reference(inv_factor, border, touched, live_count, regular):
    schur_full = jnp.diag(regular.astype(jnp.float32))
    schur_full, unused = lax.scan(add_scenario, schur_full, (inv_factor, border, touched, live_count))
    corner_factor = jnp.linalg.cholesky(schur_full[:PANEL, :PANEL])
    panel = lax.linalg.triangular_solve(corner_factor, schur_full[:, :PANEL], left_side=False, lower=True, transpose_a=True)
    return (schur_full, panel)
```

```python
import functools

import jax
import jax.numpy as jnp
from jax import lax
from jax.experimental import pallas as pl
from jax.experimental.pallas import tpu as pltpu
from jax.sharding import PartitionSpec as P

FIRST = 16384
PANEL = 1024
STEPS = 4
PIVOTS = 8
MIB = 1 << 20

SMEM = pl.BlockSpec(memory_space=pltpu.SMEM)
VMEM = pl.BlockSpec(memory_space=pltpu.VMEM)
ANY = pl.BlockSpec(memory_space=pl.ANY)


def gram_kernel(
    groups, block, group_size, ratio, touched_ref, live_ref, regular_ref, inv_ref, border_ref,
    main_ref, panel_ref, corner_ref, border_scr, scaled_scr,
):
    step = pl.program_id(0)
    rows = inv_ref.shape[0]

    def slot_of(group):
        slot = jnp.int32(0)
        for m in range(groups):
            slot = jnp.where(touched_ref[0, m] // group_size == group, m, slot)
        return slot

    @pl.when(step == 0)
    def order_slots():
        for group in range(groups):
            slot = slot_of(group)
            columns = border_ref[:, pl.ds(pl.multiple_of(slot * block, block), block)]
            keep = (slot < live_ref[0]).astype(jnp.float32)
            border_scr[:, group * block:(group + 1) * block] = columns * keep.astype(columns.dtype)

    scaled = jnp.dot(inv_ref[...], border_scr[...], preferred_element_type=jnp.float32)
    scaled_scr[pl.ds(pl.multiple_of(step * rows, rows), rows), :] = scaled.astype(scaled_scr.dtype)

    @pl.when(step == pl.num_programs(0) - 1)
    def finish():
        for group in range(groups):
            strip = lax.dot_general(
                scaled_scr[:, group * block:(group + 1) * block],
                scaled_scr[...],
                (((0,), (0,)), ((), ())),
                preferred_element_type=jnp.float32,
            )
            for other in range(groups):
                main_ref[group * groups + other] = strip[:, other * block:(other + 1) * block]
        place = lax.axis_index("scen") // ratio
        for k in range(groups):
            panel_ref[k] = main_ref[(place ^ k) * groups]
        corner_ref[:block, :] = main_ref[0]
        is_root = (lax.axis_index("scen") == 0) & (lax.axis_index("tile") == 0)
        batch = corner_ref.shape[0] - block - 8
        corner_ref[block:block + batch, :] = regular_ref[:batch, :] * is_root.astype(jnp.float32)
        lane = lax.broadcasted_iota(jnp.int32, (8, block), 1)
        labels = jnp.zeros((8, block), jnp.float32)
        for group in range(groups):
            slot = slot_of(group)
            label = jnp.where(slot < live_ref[0], touched_ref[0, slot], -1)
            labels = jnp.where(lane == group, label.astype(jnp.float32), labels)
        corner_ref[block + batch:, :] = labels


def pivot_rows(rows, start, lane):
    count = len(rows)
    block = lane.shape[1]
    entry = {}
    for a in range(count):
        for b in range(a, count):
            entry[a, b] = jnp.broadcast_to(rows[a][:, b:b + 1], lane.shape)
    lower = {}
    for a in range(count):
        lower[a, a] = 1.0 / entry[a, a]
        for b in range(a + 1, count):
            lower[b, a] = entry[a, b] * lower[a, a]
            for c in range(b, count):
                entry[b, c] = entry[b, c] - lower[b, a] * entry[a, c]
    whole, mults, pivots, done = [], [], [], []
    for a in range(count):
        row = rows[a]
        for b in range(a):
            row = jnp.where(lane == b, 0.0, row) - lower[a, b] * whole[b]
        mults.append(row * lower[a, a])
        whole.append(jnp.where(lane == a, 1.0, row))
        pivots.append(jnp.where((lane > a) & (lane < count), 0.0, whole[a]))
        keep = (lane <= a) | (lane >= block - start)
        done.append(jnp.where(keep, whole[a] * lax.rsqrt(entry[a, a]), 0.0))
    return mults, pivots, done


def split_three(value):
    high = value.astype(jnp.bfloat16).astype(jnp.float32)
    rest = value - high
    middle = rest.astype(jnp.bfloat16).astype(jnp.float32)
    return high, middle, rest - middle


def factor_kernel(batch, block, label_ref, *refs):
    *piece_refs, out_ref, sum_scr, mult_scr, pivot_scr = refs
    sum_scr[...] = jnp.zeros_like(sum_scr)
    diagonal = jnp.zeros((batch, block), jnp.float32)
    base = 0
    for piece in piece_refs:
        for i in range(piece.shape[0]):
            diagonal = diagonal + piece[i, block:block + batch, :]

        def add_one(i, unused, piece=piece, base=base):
            label = label_ref[base + i, 0]

            @pl.when((label >= 0) & (label < batch))
            def add():
                at = pl.ds(pl.multiple_of(label * block, block), block)
                sum_scr[at, :] += piece[i, :block, :]

            return unused

        lax.fori_loop(0, piece.shape[0], add_one, 0)
        base += piece.shape[0]
    row_id = lax.broadcasted_iota(jnp.int32, (block, block), 0)
    col_id = lax.broadcasted_iota(jnp.int32, (block, block), 1)
    for j in range(batch):
        at = slice(j * block, (j + 1) * block)
        sum_scr[at, :] += jnp.where(row_id == col_id, diagonal[j:j + 1, :], 0.0)
    lane = lax.broadcasted_iota(jnp.int32, (batch, block), 1)

    def eliminate(turn, unused):
        start = turn * PIVOTS
        rows = [
            pltpu.roll(sum_scr[pl.ds(start + a, batch, stride=block), :], block - start, 1)
            for a in range(PIVOTS)
        ]
        mults, pivots, done = pivot_rows(rows, start, lane)
        below = (lane >= PIVOTS) & (lane < block - start)
        for a in range(PIVOTS):
            at = slice(a * batch, (a + 1) * batch)
            out_ref[pl.ds(start + a, batch, stride=block), :] = pltpu.roll(done[a], start, 1)
            mult_scr[at, :] = pltpu.roll(jnp.where(below, mults[a], 0.0), start, 1)
            pivot_scr[at, :] = pltpu.roll(pivots[a], start, 1)
        pivot_lane = (col_id >= start) & (col_id < start + PIVOTS)
        for j in range(batch):
            high, middle, low = split_three(mult_scr[pl.ds(j, PIVOTS, stride=batch), :])
            left = jnp.concatenate([high, high, middle, high, middle, low])
            high, middle, low = split_three(pivot_scr[pl.ds(j, PIVOTS, stride=batch), :])
            right = jnp.concatenate([high, middle, high, low, middle, high])
            change = lax.dot_general(
                left.astype(jnp.bfloat16), right.astype(jnp.bfloat16),
                (((0,), (0,)), ((), ())), preferred_element_type=jnp.float32,
            )
            at = slice(j * block, (j + 1) * block)
            sum_scr[at, :] = jnp.where(pivot_lane, 0.0, sum_scr[at, :]) - change
        return unused

    lax.fori_loop(0, block // PIVOTS, eliminate, 0)


def split(value):
    high = value.astype(jnp.bfloat16)
    low = (value - high.astype(jnp.float32)).astype(jnp.bfloat16)
    return high, low


def times_transposed(left, right):
    dims = (((1,), (1,)), ((), ()))
    left_high, left_low = split(left)
    right_high, right_low = split(right)
    dot = functools.partial(
        lax.dot_general, dimension_numbers=dims, preferred_element_type=jnp.float32
    )
    return dot(left_high, right_high) + (dot(left_high, right_low) + dot(left_low, right_high))


def panel_kernel(batch, block, ratio, label_ref, regular_ref, inverse_ref, *refs):
    *piece_refs, out_ref, sum_scr = refs
    share = out_ref.shape[0]
    tile_count = lax.axis_size("tile")
    first_row = (lax.axis_index("scen") * tile_count + lax.axis_index("tile")) * share
    place = lax.axis_index("scen") // ratio
    sum_scr[...] = jnp.zeros_like(sum_scr)
    base = 0
    for piece in piece_refs:

        def add_one(i, unused, piece=piece, base=base):
            row = label_ref[base + i, place] * block
            column = label_ref[base + i, 0]
            wanted = (column >= 0) & (column < batch) & (row >= 0)
            if share >= block:
                wanted = wanted & (row >= first_row) & (row < first_row + share)
            else:
                wanted = wanted & (row <= first_row) & (first_row < row + block)

            @pl.when(wanted)
            def add():
                if share >= block:
                    at = pl.multiple_of(row - first_row, block)
                    sum_scr[column, pl.ds(at, block), :] += piece[i]
                else:
                    at = pl.multiple_of(first_row - row, share)
                    sum_scr[column] += piece[i, pl.ds(at, share), :]

            return unused

        lax.fori_loop(0, piece.shape[0], add_one, 0)
        base += piece.shape[0]

    @pl.when(first_row < batch * block)
    def add_diagonal():
        for j in range(batch):
            row_id = first_row + lax.broadcasted_iota(jnp.int32, (share, block), 0)
            col_id = j * block + lax.broadcasted_iota(jnp.int32, (share, block), 1)
            sum_scr[j] += jnp.where(row_id == col_id, regular_ref[j:j + 1, :], 0.0)

    for j in range(batch):
        product = times_transposed(sum_scr[j], inverse_ref[j * block:(j + 1) * block, :])
        out_ref[:, j * block:(j + 1) * block] = product


def scatter_kernel(block, ratio, label_ref, regular_ref, *refs):
    *piece_refs, back_ref, out_ref, sum_scr, owner_ref, spot_ref, sems = refs
    row_id = lax.broadcasted_iota(jnp.int32, (block, block), 0)
    col_id = lax.broadcasted_iota(jnp.int32, (block, block), 1)
    scen, tile = lax.axis_index("scen"), lax.axis_index("tile")
    tile_count = lax.axis_size("tile")
    place = scen // ratio
    tall, wide = out_ref.shape[0] // block, out_ref.shape[1] // block

    def clear(i, unused):
        owner_ref[i] = -1
        return unused

    lax.fori_loop(0, tall * wide, clear, 0)

    def copy(i):
        spot = spot_ref[i]
        row = pl.multiple_of(spot // wide * block, block)
        column = pl.multiple_of(spot % wide * block, block)
        return pltpu.make_async_copy(
            sum_scr.at[i], out_ref.at[pl.ds(row, block), pl.ds(column, block)], sems.at[i]
        )

    base = 0
    for piece in piece_refs:

        def add_one(i, unused, piece=piece, base=base):
            sender = base + ((i % tile_count) ^ tile) * (piece.shape[0] // tile_count) + ((i // tile_count) ^ place)
            row, column = label_ref[sender, place], label_ref[sender, tile]
            inside = (row >= scen * tall) & (row < (scen + 1) * tall) & (column >= 0)
            spot = jnp.where(inside, (row - scen * tall) * wide + column - tile * wide, 0)
            owner = owner_ref[spot]
            spot_ref[base + i] = jnp.where(inside & (owner < 0), spot, -1)

            @pl.when(inside & (owner < 0))
            def put():
                owner_ref[spot] = base + i
                values = regular_ref[pl.ds(spot // wide, 1), :] * (row == column).astype(jnp.float32)
                sum_scr[base + i] = piece[i] + jnp.where(row_id == col_id, values, 0.0)

            @pl.when(inside & (owner >= 0))
            def add():
                sum_scr[owner] += piece[i]

            return unused

        lax.fori_loop(0, piece.shape[0], add_one, 0)
        base += piece.shape[0]

    def start_one(i, unused):
        @pl.when(spot_ref[i] >= 0)
        def start():
            copy(i).start()

        return unused

    def wait_one(i, unused):
        @pl.when(spot_ref[i] >= 0)
        def wait():
            copy(i).wait()

        return unused

    lax.fori_loop(0, base, start_one, 0)
    lax.fori_loop(0, base, wait_one, 0)


def local(inv_factor, border, touched, live_count, regular):
    scen_count = lax.axis_size("scen")
    tile_count = lax.axis_size("tile")
    scen_index = lax.axis_index("scen")
    tile_index = lax.axis_index("tile")
    local_count, order_size, width = border.shape
    groups = touched.shape[1]
    block = width // groups
    block_total = FIRST // block
    group_size = block_total // groups
    batch = PANEL // block
    ratio = scen_count // groups
    row_span = block_total // scen_count
    row_share = FIRST // (scen_count * tile_count)
    assert local_count == 1 and tile_count == groups and scen_count == groups * ratio
    assert batch <= group_size and batch * block <= regular.shape[0]
    both = ("scen", "tile")
    regular_rows = regular.reshape(-1, block)

    main, strip, corner = pl.pallas_call(
        functools.partial(gram_kernel, groups, block, group_size, ratio),
        grid=(STEPS,),
        in_specs=[
            SMEM, SMEM,
            pl.BlockSpec(regular_rows.shape, lambda i: (0, 0)),
            pl.BlockSpec((order_size // STEPS, order_size), lambda i: (i, 0)),
            pl.BlockSpec((order_size, width), lambda i: (0, 0)),
        ],
        out_specs=[
            pl.BlockSpec((groups * groups, block, block), lambda i: (0, 0, 0)),
            pl.BlockSpec((groups, block, block), lambda i: (0, 0, 0)),
            pl.BlockSpec((block + batch + 8, block), lambda i: (0, 0)),
        ],
        out_shape=[
            jax.ShapeDtypeStruct((groups * groups, block, block), jnp.float32),
            jax.ShapeDtypeStruct((groups, block, block), jnp.float32),
            jax.ShapeDtypeStruct((block + batch + 8, block), jnp.float32),
        ],
        scratch_shapes=[
            pltpu.VMEM((order_size, width), border.dtype),
            pltpu.VMEM((order_size, width), border.dtype),
        ],
        compiler_params=pltpu.CompilerParams(vmem_limit_bytes=56 * MIB),
    )(touched, live_count, regular_rows, inv_factor[0], border[0])

    def along_place(array, k):
        pairs = [(s, (s // ratio ^ k) * ratio + s % ratio) for s in range(scen_count)]
        return lax.ppermute(array, "scen", pairs)

    def along_tile(array, k):
        return lax.ppermute(array, "tile", [(t, t ^ k) for t in range(tile_count)])

    def along_part(array, k):
        pairs = [(s, s // ratio * ratio + (s % ratio ^ k)) for s in range(scen_count)]
        return lax.ppermute(array, "scen", pairs)

    def gather_plane(array):
        here = [array] + [along_tile(array, k) for k in range(1, tile_count)]
        here = jnp.concatenate(here)
        return [here] + [along_part(here, k) for k in range(1, ratio)]

    corners = [corner] + [along_place(corner, k) for k in range(1, groups)]
    corners = gather_plane(jnp.stack(corners))
    strips = [strip[0]] + [along_place(strip[k], k) for k in range(1, groups)]
    strips = gather_plane(jnp.stack(strips))
    teams = [
        [(z * ratio + c) * tile_count + t for z in range(groups) for t in range(tile_count)]
        for c in range(ratio)
    ]
    blocks = lax.all_to_all(main, both, 0, 0, tiled=True, axis_index_groups=teams)
    blocks = [blocks] + [along_part(blocks, k) for k in range(1, ratio)]

    labels = jnp.concatenate([piece[:, block + batch, :groups] for piece in corners]).astype(jnp.int32)

    tall, wide = row_span * block, group_size * block
    row_id = scen_index * tall + lax.broadcasted_iota(jnp.int32, (tall, wide), 0)
    col_id = tile_index * wide + lax.broadcasted_iota(jnp.int32, (tall, wide), 1)
    background = jnp.where(row_id == col_id, regular[:, None], 0.0)

    inverse = pl.pallas_call(
        functools.partial(factor_kernel, batch, block),
        in_specs=[SMEM] + [VMEM] * len(corners),
        out_specs=VMEM,
        out_shape=jax.ShapeDtypeStruct((batch * block, block), jnp.float32),
        scratch_shapes=[
            pltpu.VMEM((batch * block, block), jnp.float32),
            pltpu.VMEM((batch * PIVOTS, block), jnp.float32),
            pltpu.VMEM((batch * PIVOTS, block), jnp.float32),
        ],
        compiler_params=pltpu.CompilerParams(vmem_limit_bytes=48 * MIB),
    )(labels, *corners)

    panel = pl.pallas_call(
        functools.partial(panel_kernel, batch, block, ratio),
        in_specs=[SMEM, VMEM, VMEM] + [VMEM] * len(strips),
        out_specs=VMEM,
        out_shape=jax.ShapeDtypeStruct((row_share, batch * block), jnp.float32),
        scratch_shapes=[pltpu.VMEM((batch, row_share, block), jnp.float32)],
        compiler_params=pltpu.CompilerParams(vmem_limit_bytes=48 * MIB),
    )(labels, regular_rows, inverse, *strips)

    count = ratio * blocks[0].shape[0]
    schur = pl.pallas_call(
        functools.partial(scatter_kernel, block, ratio),
        in_specs=[SMEM, VMEM] + [VMEM] * len(blocks) + [ANY],
        out_specs=ANY,
        out_shape=jax.ShapeDtypeStruct((tall, wide), jnp.float32),
        input_output_aliases={2 + len(blocks): 0},
        scratch_shapes=[
            pltpu.VMEM((count, block, block), jnp.float32),
            pltpu.SMEM((row_span * group_size,), jnp.int32),
            pltpu.SMEM((count,), jnp.int32),
            pltpu.SemaphoreType.DMA((count,)),
        ],
        compiler_params=pltpu.CompilerParams(vmem_limit_bytes=48 * MIB),
    )(labels, regular_rows, *blocks, background)
    return (schur, panel)


def solution(mesh):
    return jax.shard_map(
        local,
        mesh=mesh,
        in_specs=(
            P(("scen", "tile"), None, None),
            P(("scen", "tile"), None, None),
            P(("scen", "tile"), None),
            P(("scen", "tile")),
            P("scen"),
        ),
        out_specs=(P("scen", "tile"), P(("scen", "tile"), None)),
        check_vma=False,
    )
```

```python
import functools
import math

import jax
import jax.numpy as jnp
from jax import lax
from jax.experimental import pallas as pl
from jax.experimental.pallas import tpu as pltpu
from jax.sharding import PartitionSpec as P

FIRST = 16384
PANEL = 1024
PIVOTS = 8
ZEROS = 64
MIB = 1 << 20

SMEM = pl.BlockSpec(memory_space=pltpu.SMEM)
VMEM = pl.BlockSpec(memory_space=pltpu.VMEM)
ANY = pl.BlockSpec(memory_space=pl.ANY)
HBM = pl.BlockSpec(memory_space=pltpu.HBM)


def gram(left, right):
    return lax.dot_general(left, right, (((0,), (0,)), ((), ())), preferred_element_type=jnp.float32)


def fill(zero_scr, back_ref, sems):
    tall = zero_scr.shape[0]
    zero_scr[...] = jnp.zeros_like(zero_scr)
    copies = [
        pltpu.make_async_copy(zero_scr, back_ref.at[i * tall:(i + 1) * tall], sems.at[i])
        for i in range(back_ref.shape[0] // tall)
    ]
    for copy in copies:
        copy.start()
    return copies


def first_kernel(
    groups, block, group_size, ratio, touched_ref, live_ref, regular_ref, inv_ref, border_ref,
    scaled_ref, *refs,
):
    *first_refs, inv_scr, border_scr, column_scr, inv_sem, border_sems = refs
    place = lax.axis_index("scen") // ratio
    copies = []
    keeps, labels = [], []
    for group in range(groups):
        slot = jnp.int32(0)
        for m in range(groups):
            slot = jnp.where(touched_ref[0, m] // group_size == group, m, slot)
        copies.append(pltpu.make_async_copy(
            border_ref.at[:, pl.ds(pl.multiple_of(slot * block, block), block)],
            border_scr.at[:, group * block:(group + 1) * block],
            border_sems.at[group],
        ))
        keeps.append(slot < live_ref[0])
        labels.append(jnp.where(slot < live_ref[0], touched_ref[0, slot], -1).astype(jnp.float32))
    copies.append(pltpu.make_async_copy(inv_ref, inv_scr, inv_sem))
    for copy in copies:
        copy.start()
    keep = jnp.concatenate(
        [jnp.broadcast_to(keep.astype(jnp.float32), (1, block)) for keep in keeps], axis=1
    )
    for copy in copies:
        copy.wait()
    scaled = jnp.dot(inv_scr[...], border_scr[...], preferred_element_type=jnp.float32)
    scaled_ref[...] = jnp.where(keep > 0.0, scaled, 0.0).astype(scaled_ref.dtype)
    strip = gram(scaled_ref[:, :block], scaled_ref[...])
    half = block // 2
    corner_rows = first_refs[0].shape[0] - block
    corner = pack_corner(groups, strip[:, :block])
    is_root = (lax.axis_index("scen") == 0) & (lax.axis_index("tile") == 0)
    root_rows = regular_ref[:corner_rows - half - 8, :] * is_root.astype(jnp.float32)
    lane = lax.broadcasted_iota(jnp.int32, (8, block), 1)
    last = corner[half:]
    for group in range(groups):
        column_scr[group] = strip[:, group * block:(group + 1) * block].T
        last = jnp.where(lane == group, labels[group], last)
    for k in range(groups):
        first_refs[k][:half] = corner[:half]
        first_refs[k][half:half + 8] = last
        first_refs[k][half + 8:corner_rows] = root_rows
        first_refs[k][corner_rows:] = column_scr[place ^ k]


def main_kernel(groups, block, scaled_ref, main_ref):
    for group in range(groups):
        strip = gram(scaled_ref[:, group * block:(group + 1) * block], scaled_ref[...])
        for other in range(groups):
            main_ref[group * groups + other] = strip[:, other * block:(other + 1) * block]


def pack_corner(groups, whole):
    block = whole.shape[0]
    half = block // 2
    assert groups <= half
    row_id = lax.broadcasted_iota(jnp.int32, (half, block), 0)
    col_id = lax.broadcasted_iota(jnp.int32, (half, block), 1)
    upper, lower = whole[:half], whole[half:]
    body = jnp.where(col_id >= row_id, upper, pltpu.roll(lower, half, 1))
    ends = jnp.sum(jnp.where(col_id == row_id + half, lower, 0.0), axis=0, keepdims=True)
    return jnp.concatenate([body, jnp.broadcast_to(ends, (8, block))])


def unpack_upper(block, packed, ends):
    half = block // 2
    row_id = lax.broadcasted_iota(jnp.int32, (half, block), 0)
    col_id = lax.broadcasted_iota(jnp.int32, (half, block), 1)
    low = jnp.where(col_id < row_id, packed, 0.0)
    turned = jnp.concatenate([low, jnp.zeros_like(low)]).T[:half]
    lower = pltpu.roll(turned, half, 1) + jnp.where(col_id == row_id + half, ends, 0.0)
    return jnp.concatenate([packed, lower])


def pivot_rows(rows, start, lane):
    count = len(rows)
    entry = {}
    for b in range(count):
        at = jnp.full(lane.shape, start + b, jnp.int32)
        for a in range(b + 1):
            entry[a, b] = jnp.take_along_axis(rows[a], at, axis=1, mode="promise_in_bounds")
    lower = {}
    for a in range(count):
        lower[a, a] = 1.0 / entry[a, a]
        for b in range(a + 1, count):
            lower[b, a] = entry[a, b] * lower[a, a]
            for c in range(b, count):
                entry[b, c] = entry[b, c] - lower[b, a] * entry[a, c]
    whole, mults, pivots, done = [], [], [], []
    for a in range(count):
        row = rows[a]
        for b in range(a):
            row = jnp.where(lane == start + b, 0.0, row) - lower[a, b] * whole[b]
        mults.append(jnp.where(lane >= start + count, row * lower[a, a], 0.0))
        whole.append(jnp.where(lane == start + a, 1.0, row))
        pivots.append(jnp.where((lane > start + a) & (lane < start + count), 0.0, whole[a]))
        done.append(jnp.where(lane <= start + a, whole[a] * lax.rsqrt(entry[a, a]), 0.0))
    return mults, pivots, done


def split_three(value):
    high = value.astype(jnp.bfloat16).astype(jnp.float32)
    rest = value - high
    middle = rest.astype(jnp.bfloat16).astype(jnp.float32)
    return high, middle, rest - middle


def factor_kernel(batch, block, ratio, share, *refs):
    (*piece_refs, out_ref, back_ref, plan_ref, spot_ref,
     packed_scr, sum_scr, mult_scr, pivot_scr, zero_scr, label_scr, owner_scr, sems) = refs
    half = block // 2
    scen, tile = lax.axis_index("scen"), lax.axis_index("tile")
    tile_count = lax.axis_size("tile")
    place = scen // ratio
    tall, wide = back_ref.shape[0] // block, back_ref.shape[1] // block
    count, groups = label_scr.shape
    turns = block // PIVOTS
    per_turn = -(-count // turns)
    assert count % turns == 0
    nowhere = tall * wide
    device_row = (scen * tile_count + tile) * share

    def claim(i):
        part, sent = i // (tile_count * groups), i % (tile_count * groups)
        sender = part * (tile_count * groups) + ((sent % tile_count) ^ tile) * groups + ((sent // tile_count) ^ place)
        row, column = label_scr[sender, place], label_scr[sender, tile]
        inside = (row >= scen * tall) & (row < (scen + 1) * tall) & (column >= 0)
        spot = jnp.where(inside, (row - scen * tall) * wide + column - tile * wide, nowhere)
        owner = owner_scr[spot]
        owner = jnp.where(inside, jnp.where(owner < 0, i, owner), -1)
        owner_scr[spot] = owner
        plan_ref[0, i] = owner
        spot_ref[i] = jnp.where(owner == i, spot, -1)
        row, column = label_scr[i, place] * block, label_scr[i, 0]
        wanted = (column >= 0) & (column < batch) & (row >= 0)
        wanted = wanted & (row < device_row + share) & (device_row < row + block)
        plan_ref[1, i] = jnp.where(wanted, jnp.maximum(row - device_row, 0) // block * batch + column, -1)

    copies = fill(zero_scr, back_ref, sems)
    for i in range(nowhere + 1):
        owner_scr[i] = -1
    for i in range(tall):
        column = scen * tall + i - tile * wide
        spot = jnp.where((column >= 0) & (column < wide), i * wide + column, nowhere)
        owner_scr[spot] = count + i
        spot_ref[count + i] = jnp.where(spot < nowhere, spot, -1)
    packed_scr[...] = jnp.zeros_like(packed_scr)
    diagonal = jnp.zeros((batch, block), jnp.float32)
    base = 0
    for piece in piece_refs:
        for i in range(piece.shape[0]):
            diagonal = diagonal + piece[i, half + 8:half + 8 + batch, :]
            for group in range(groups):
                label_scr[base + i, group] = piece[i, half, group].astype(jnp.int32)
        base += piece.shape[0]
    base = 0
    for piece in piece_refs:

        def add_one(i, unused, piece=piece, base=base):
            label = label_scr[base + i, 0]

            @pl.when((label >= 0) & (label < batch))
            def add():
                packed_scr[label] += piece[i, :half + 8, :]

            return unused

        lax.fori_loop(0, piece.shape[0], add_one, 0)
        base += piece.shape[0]
    row_id = lax.broadcasted_iota(jnp.int32, (block, block), 0)
    col_id = lax.broadcasted_iota(jnp.int32, (block, block), 1)
    for j in range(batch):
        values = unpack_upper(block, packed_scr[j, :half], packed_scr[j, half:half + 1])
        sum_scr[j * block:(j + 1) * block, :] = values + jnp.where(row_id == col_id, diagonal[j:j + 1, :], 0.0)
    lane = lax.broadcasted_iota(jnp.int32, (batch, block), 1)

    def eliminate(turn, unused):
        start = turn * PIVOTS
        rows = [sum_scr[pl.ds(start + a, batch, stride=block), :] for a in range(PIVOTS)]
        mults, pivots, done = pivot_rows(rows, start, lane)
        for a in range(PIVOTS):
            at = slice(a * batch, (a + 1) * batch)
            out_ref[pl.ds(start + a, batch, stride=block), :] = done[a]
            mult_scr[at, :] = mults[a]
            pivot_scr[at, :] = pivots[a]
        for n in range(per_turn):
            claim(turn * per_turn + n)
        pivot_lane = (col_id >= start) & (col_id < start + PIVOTS)
        for j in range(batch):
            high, middle, low = split_three(mult_scr[pl.ds(j, PIVOTS, stride=batch), :])
            left = jnp.concatenate([high, high, middle, high, middle, low])
            high, middle, low = split_three(pivot_scr[pl.ds(j, PIVOTS, stride=batch), :])
            right = jnp.concatenate([high, middle, high, low, middle, high])
            change = lax.dot_general(
                left.astype(jnp.bfloat16), right.astype(jnp.bfloat16),
                (((0,), (0,)), ((), ())), preferred_element_type=jnp.float32,
            )
            at = slice(j * block, (j + 1) * block)
            sum_scr[at, :] = jnp.where(pivot_lane, 0.0, sum_scr[at, :]) - change
        return unused

    lax.fori_loop(0, turns, eliminate, 0)
    for copy in copies:
        copy.wait()


def split(value):
    high = value.astype(jnp.bfloat16)
    low = (value - high.astype(jnp.float32)).astype(jnp.bfloat16)
    return high, low


def panel_kernel(batch, block, plan_ref, regular_ref, inverse_ref, *refs):
    *piece_refs, out_ref, sum_scr, out_scr, sems = refs
    share = out_ref.shape[0]
    tall = min(share, block)
    first_row = (lax.axis_index("scen") * lax.axis_size("tile") + lax.axis_index("tile")) * share
    sum_scr[...] = jnp.zeros_like(sum_scr)
    base = 0
    for piece in piece_refs:
        for i in range(piece.shape[0]):
            spot = plan_ref[1, base + i]

            @pl.when(spot >= 0)
            def add(piece=piece, i=i, spot=spot):
                at = pl.multiple_of(spot // batch * tall, tall)
                piece_at = pl.multiple_of(first_row % block // tall * tall, tall)
                sum_scr[spot % batch, pl.ds(at, tall), :] += piece[i, pl.ds(piece_at, tall), :]

        base += piece.shape[0]

    @pl.when(first_row < batch * block)
    def add_diagonal():
        for j in range(batch):
            row_id = first_row + lax.broadcasted_iota(jnp.int32, (share, block), 0)
            col_id = j * block + lax.broadcasted_iota(jnp.int32, (share, block), 1)
            sum_scr[j] += jnp.where(row_id == col_id, regular_ref[j:j + 1, :], 0.0)

    copies = []
    for j in range(batch):
        at = slice(j * block, (j + 1) * block)
        left = jnp.concatenate(split(sum_scr[j]), axis=1)
        high, low = split(inverse_ref[at, :])
        right = jnp.concatenate([
            jnp.concatenate([high, high], axis=1),
            jnp.concatenate([low, jnp.zeros_like(low)], axis=1),
        ])
        product = lax.dot_general(
            left, right, (((1,), (1,)), ((), ())), preferred_element_type=jnp.float32
        )
        out_scr[j] = product[:, :block] + product[:, block:]
        copies.append(pltpu.make_async_copy(out_scr.at[j], out_ref.at[:, at], sems.at[j]))
        copies[-1].start()
    for copy in copies:
        copy.wait()


def scatter_kernel(block, plan_ref, spot_ref, regular_ref, *refs):
    *piece_refs, back_ref, out_ref, sum_scr, sems = refs
    row_id = lax.broadcasted_iota(jnp.int32, (block, block), 0)
    col_id = lax.broadcasted_iota(jnp.int32, (block, block), 1)
    tall, wide = out_ref.shape[0] // block, out_ref.shape[1] // block
    count = sum(piece.shape[0] for piece in piece_refs)

    def diagonal_one(i, unused):
        @pl.when(spot_ref[count + i] >= 0)
        def put():
            sum_scr[count + i] = jnp.where(row_id == col_id, regular_ref[pl.ds(i, 1), :], 0.0)

        return unused

    lax.fori_loop(0, tall, diagonal_one, 0)
    base = 0
    for piece in piece_refs:

        def add_one(i, unused, piece=piece, base=base):
            owner = plan_ref[0, base + i]

            @pl.when(owner == base + i)
            def put():
                sum_scr[owner] = piece[i]

            @pl.when((owner >= 0) & (owner != base + i))
            def add():
                sum_scr[owner] += piece[i]

            return unused

        lax.fori_loop(0, piece.shape[0], add_one, 0)
        base += piece.shape[0]

    def copy(i):
        spot = spot_ref[i]
        row = pl.multiple_of(spot // wide * block, block)
        column = pl.multiple_of(spot % wide * block, block)
        return pltpu.make_async_copy(
            sum_scr.at[i], out_ref.at[pl.ds(row, block), pl.ds(column, block)], sems.at[i]
        )

    def start_one(i, unused):
        @pl.when(spot_ref[i] >= 0)
        def start():
            copy(i).start()

        return unused

    def wait_one(i, unused):
        @pl.when(spot_ref[i] >= 0)
        def wait():
            copy(i).wait()

        return unused

    lax.fori_loop(0, count + tall, start_one, 0)
    lax.fori_loop(0, count + tall, wait_one, 0)


def limit(*held):
    size = sum(math.prod(one.shape) * jnp.dtype(one.dtype).itemsize for one in held)
    return pltpu.CompilerParams(vmem_limit_bytes=min(size + 4 * MIB, 60 * MIB))


def local(inv_factor, border, touched, live_count, regular):
    scen_count = lax.axis_size("scen")
    tile_count = lax.axis_size("tile")
    scen_index = lax.axis_index("scen")
    tile_index = lax.axis_index("tile")
    local_count, order_size, width = border.shape
    groups = touched.shape[1]
    block = width // groups
    block_total = FIRST // block
    group_size = block_total // groups
    batch = PANEL // block
    ratio = scen_count // groups
    row_span = block_total // scen_count
    row_share = FIRST // (scen_count * tile_count)
    assert local_count == 1 and tile_count == groups and scen_count == groups * ratio
    assert batch <= group_size and batch * block <= regular.shape[0]
    corner_rows = block // 2 + 8 + batch
    both = ("scen", "tile")
    regular_rows = regular.reshape(-1, block)

    tall, wide = row_span * block, group_size * block
    zeros = [pltpu.VMEM((ZEROS, wide), jnp.float32), pltpu.SemaphoreType.DMA((tall // ZEROS,))]

    scaled, *first = pl.pallas_call(
        functools.partial(first_kernel, groups, block, group_size, ratio),
        in_specs=[SMEM, SMEM, VMEM, HBM, HBM],
        out_specs=[VMEM] * (groups + 1),
        out_shape=[jax.ShapeDtypeStruct((order_size, width), border.dtype)]
        + [jax.ShapeDtypeStruct((corner_rows + block, block), jnp.float32)] * groups,
        scratch_shapes=[
            pltpu.VMEM((order_size, order_size), inv_factor.dtype),
            pltpu.VMEM((order_size, width), border.dtype),
            pltpu.VMEM((groups, block, block), jnp.float32),
            pltpu.SemaphoreType.DMA,
            pltpu.SemaphoreType.DMA((groups,)),
        ],
        compiler_params=pltpu.CompilerParams(vmem_limit_bytes=60 * MIB),
    )(touched, live_count, regular_rows, inv_factor[0], border[0])
    main = pl.pallas_call(
        functools.partial(main_kernel, groups, block),
        in_specs=[VMEM],
        out_specs=VMEM,
        out_shape=jax.ShapeDtypeStruct((groups * groups, block, block), jnp.float32),
        compiler_params=limit(scaled, jax.ShapeDtypeStruct((groups * groups, block, block), jnp.float32)),
    )(scaled)
    def along_place(array, k):
        pairs = [(s, (s // ratio ^ k) * ratio + s % ratio) for s in range(scen_count)]
        return lax.ppermute(array, "scen", pairs)

    def along_tile(array, k):
        return lax.ppermute(array, "tile", [(t, t ^ k) for t in range(tile_count)])

    def along_part(array, k):
        pairs = [(s, s // ratio * ratio + (s % ratio ^ k)) for s in range(scen_count)]
        return lax.ppermute(array, "scen", pairs)

    def along_tiles(array):
        return [array] + [along_tile(array, k) for k in range(1, tile_count)]

    def along_parts(pieces):
        return pieces + [along_part(piece, k) for k in range(1, ratio) for piece in pieces]

    firsts = [first[0]] + [along_place(first[k], k) for k in range(1, groups)]
    corners = along_tiles(jnp.stack([piece[:corner_rows] for piece in firsts]))
    corners = along_parts(corners)
    strips = along_tiles(jnp.stack([piece[corner_rows:] for piece in firsts]))
    teams = [
        [(z * ratio + c) * tile_count + t for z in range(groups) for t in range(tile_count)]
        for c in range(ratio)
    ]
    blocks = lax.all_to_all(main, both, 0, 0, tiled=True, axis_index_groups=teams)
    count = scen_count * tile_count
    scratch = [
        pltpu.VMEM((batch, block // 2 + 8, block), jnp.float32),
        pltpu.VMEM((batch * block, block), jnp.float32),
        pltpu.VMEM((batch * PIVOTS, block), jnp.float32),
        pltpu.VMEM((batch * PIVOTS, block), jnp.float32),
        zeros[0],
    ]
    inverse, background, plan, spots = pl.pallas_call(
        functools.partial(factor_kernel, batch, block, ratio, row_share),
        in_specs=[VMEM] * len(corners),
        out_specs=[VMEM, ANY, SMEM, SMEM],
        out_shape=[
            jax.ShapeDtypeStruct((batch * block, block), jnp.float32),
            jax.ShapeDtypeStruct((tall, wide), jnp.float32),
            jax.ShapeDtypeStruct((2, count), jnp.int32),
            jax.ShapeDtypeStruct((count + row_span,), jnp.int32),
        ],
        scratch_shapes=scratch + [
            pltpu.SMEM((count, groups), jnp.int32),
            pltpu.SMEM((row_span * group_size + 1,), jnp.int32),
            zeros[1],
        ],
        compiler_params=limit(*corners, *scratch),
    )(*corners)

    strips, inverse = lax.optimization_barrier((strips, inverse))
    strips = along_parts(strips)
    blocks, inverse = lax.optimization_barrier((blocks, inverse))
    blocks = along_parts([blocks])

    total = pltpu.VMEM((count + row_span, block, block), jnp.float32)
    schur = pl.pallas_call(
        functools.partial(scatter_kernel, block),
        in_specs=[SMEM, SMEM, VMEM] + [VMEM] * len(blocks) + [ANY],
        out_specs=ANY,
        out_shape=jax.ShapeDtypeStruct((tall, wide), jnp.float32),
        input_output_aliases={3 + len(blocks): 0},
        scratch_shapes=[total, pltpu.SemaphoreType.DMA((count + row_span,))],
        compiler_params=limit(*blocks, total),
    )(plan, spots, regular_rows, *blocks, background)
    strips, schur = lax.optimization_barrier((strips, schur))
    sums = [pltpu.VMEM((batch, row_share, block), jnp.float32)] * 2
    panel = pl.pallas_call(
        functools.partial(panel_kernel, batch, block),
        in_specs=[SMEM, VMEM, VMEM] + [VMEM] * len(strips),
        out_specs=ANY,
        out_shape=jax.ShapeDtypeStruct((row_share, batch * block), jnp.float32),
        scratch_shapes=sums + [pltpu.SemaphoreType.DMA((batch,))],
        compiler_params=limit(*strips, *sums),
    )(plan, regular_rows, inverse, *strips)
    return (schur, panel)


def solution(mesh):
    return jax.shard_map(
        local,
        mesh=mesh,
        in_specs=(
            P(("scen", "tile"), None, None),
            P(("scen", "tile"), None, None),
            P(("scen", "tile"), None),
            P(("scen", "tile")),
            P("scen"),
        ),
        out_specs=(P("scen", "tile"), P(("scen", "tile"), None)),
        check_vma=False,
    )
```

```python
import functools
import math

import jax
import jax.numpy as jnp
from jax import lax
from jax.experimental import pallas as pl
from jax.experimental.pallas import tpu as pltpu
from jax.sharding import PartitionSpec as P

FIRST = 16384
PANEL = 1024
PIVOTS = 8
ZEROS = 64
EARLY = 0.375
MIB = 1 << 20

SMEM = pl.BlockSpec(memory_space=pltpu.SMEM)
VMEM = pl.BlockSpec(memory_space=pltpu.VMEM)
ANY = pl.BlockSpec(memory_space=pl.ANY)
HBM = pl.BlockSpec(memory_space=pltpu.HBM)


def gram(left, right):
    return lax.dot_general(left, right, (((0,), (0,)), ((), ())), preferred_element_type=jnp.float32)


def fill(zero_scr, back_ref, sems, first, last):
    tall = zero_scr.shape[0]
    zero_scr[...] = jnp.zeros_like(zero_scr)
    copies = [
        pltpu.make_async_copy(zero_scr, back_ref.at[i * tall:(i + 1) * tall], sems.at[i])
        for i in range(first, last)
    ]
    for copy in copies:
        copy.start()
    return copies


def first_kernel(
    groups, block, group_size, ratio, touched_ref, live_ref, regular_ref, inv_ref, border_ref,
    main_ref, *refs,
):
    *first_refs, scaled_ref, inv_scr, border_scr, column_scr, inv_sem, border_sems = refs
    place = lax.axis_index("scen") // ratio
    copies = []
    keeps, labels = [], []
    for group in range(groups):
        slot = jnp.int32(0)
        for m in range(groups):
            slot = jnp.where(touched_ref[0, m] // group_size == group, m, slot)
        copies.append(pltpu.make_async_copy(
            border_ref.at[:, pl.ds(pl.multiple_of(slot * block, block), block)],
            border_scr.at[:, group * block:(group + 1) * block],
            border_sems.at[group],
        ))
        keeps.append(slot < live_ref[0])
        labels.append(jnp.where(slot < live_ref[0], touched_ref[0, slot], -1).astype(jnp.float32))
    copies.append(pltpu.make_async_copy(inv_ref, inv_scr, inv_sem))
    for copy in copies:
        copy.start()
    keep = jnp.concatenate(
        [jnp.broadcast_to(keep.astype(jnp.float32), (1, block)) for keep in keeps], axis=1
    )
    for copy in copies:
        copy.wait()
    scaled = jnp.dot(inv_scr[...], border_scr[...], preferred_element_type=jnp.float32)
    scaled_ref[...] = jnp.where(keep > 0.0, scaled, 0.0).astype(scaled_ref.dtype)
    strip = gram(scaled_ref[:, :block], scaled_ref[...])
    half = block // 2
    corner_rows = first_refs[0].shape[0] - block
    corner = pack_corner(groups, strip[:, :block])
    is_root = (lax.axis_index("scen") == 0) & (lax.axis_index("tile") == 0)
    root_rows = regular_ref[:corner_rows - half - 8, :] * is_root.astype(jnp.float32)
    lane = lax.broadcasted_iota(jnp.int32, (8, block), 1)
    last = corner[half:]
    for group in range(groups):
        column_scr[group] = strip[:, group * block:(group + 1) * block].T
        last = jnp.where(lane == group, labels[group], last)
    for k in range(groups):
        first_refs[k][:half] = corner[:half]
        first_refs[k][half:half + 8] = last
        first_refs[k][half + 8:corner_rows] = root_rows
        first_refs[k][corner_rows:] = column_scr[place ^ k]
    for group in range(groups):
        if group > 0:
            strip = gram(scaled_ref[:, group * block:(group + 1) * block], scaled_ref[...])
        for other in range(groups):
            main_ref[group * groups + other] = strip[:, other * block:(other + 1) * block]


def fill_kernel(early, after_ref, back_ref, zero_scr, sems):
    for copy in fill(zero_scr, back_ref, sems, 0, early):
        copy.wait()


def pack_corner(groups, whole):
    block = whole.shape[0]
    half = block // 2
    assert groups <= half
    row_id = lax.broadcasted_iota(jnp.int32, (half, block), 0)
    col_id = lax.broadcasted_iota(jnp.int32, (half, block), 1)
    upper, lower = whole[:half], whole[half:]
    body = jnp.where(col_id >= row_id, upper, pltpu.roll(lower, half, 1))
    ends = jnp.sum(jnp.where(col_id == row_id + half, lower, 0.0), axis=0, keepdims=True)
    return jnp.concatenate([body, jnp.broadcast_to(ends, (8, block))])


def unpack_upper(block, packed, ends):
    half = block // 2
    row_id = lax.broadcasted_iota(jnp.int32, (half, block), 0)
    col_id = lax.broadcasted_iota(jnp.int32, (half, block), 1)
    low = jnp.where(col_id < row_id, packed, 0.0)
    turned = jnp.concatenate([low, jnp.zeros_like(low)]).T[:half]
    lower = pltpu.roll(turned, half, 1) + jnp.where(col_id == row_id + half, ends, 0.0)
    return jnp.concatenate([packed, lower])


def pivot_rows(rows, start, lane):
    count = len(rows)
    entry = {}
    for b in range(count):
        at = jnp.full(lane.shape, start + b, jnp.int32)
        for a in range(b + 1):
            entry[a, b] = jnp.take_along_axis(rows[a], at, axis=1, mode="promise_in_bounds")
    lower = {}
    for a in range(count):
        lower[a, a] = 1.0 / entry[a, a]
        for b in range(a + 1, count):
            lower[b, a] = entry[a, b] * lower[a, a]
            for c in range(b, count):
                entry[b, c] = entry[b, c] - lower[b, a] * entry[a, c]
    whole, mults, pivots, done = [], [], [], []
    for a in range(count):
        row = rows[a]
        for b in range(a):
            row = jnp.where(lane == start + b, 0.0, row) - lower[a, b] * whole[b]
        mults.append(jnp.where(lane >= start + count, row * lower[a, a], 0.0))
        whole.append(jnp.where(lane == start + a, 1.0, row))
        pivots.append(jnp.where((lane > start + a) & (lane < start + count), 0.0, whole[a]))
        done.append(jnp.where(lane <= start + a, whole[a] * lax.rsqrt(entry[a, a]), 0.0))
    return mults, pivots, done


def split_three(value):
    high = value.astype(jnp.bfloat16).astype(jnp.float32)
    rest = value - high
    middle = rest.astype(jnp.bfloat16).astype(jnp.float32)
    return high, middle, rest - middle


def factor_kernel(batch, block, ratio, share, early, *refs):
    (*piece_refs, in_ref, out_ref, back_ref, plan_ref, spot_ref,
     packed_scr, sum_scr, mult_scr, pivot_scr, zero_scr, label_scr, owner_scr, sems) = refs
    half = block // 2
    scen, tile = lax.axis_index("scen"), lax.axis_index("tile")
    tile_count = lax.axis_size("tile")
    place = scen // ratio
    tall, wide = back_ref.shape[0] // block, back_ref.shape[1] // block
    count, groups = label_scr.shape
    turns = block // PIVOTS
    per_turn = -(-count // turns)
    assert count % turns == 0
    nowhere = tall * wide
    device_row = (scen * tile_count + tile) * share

    def claim(i):
        part, sent = i // (tile_count * groups), i % (tile_count * groups)
        sender = part * (tile_count * groups) + ((sent % tile_count) ^ tile) * groups + ((sent // tile_count) ^ place)
        row, column = label_scr[sender, place], label_scr[sender, tile]
        inside = (row >= scen * tall) & (row < (scen + 1) * tall) & (column >= 0)
        spot = jnp.where(inside, (row - scen * tall) * wide + column - tile * wide, nowhere)
        owner = owner_scr[spot]
        owner = jnp.where(inside, jnp.where(owner < 0, i, owner), -1)
        owner_scr[spot] = owner
        plan_ref[0, i] = owner
        spot_ref[i] = jnp.where(owner == i, spot, -1)
        row, column = label_scr[i, place] * block, label_scr[i, 0]
        wanted = (column >= 0) & (column < batch) & (row >= 0)
        wanted = wanted & (row < device_row + share) & (device_row < row + block)
        plan_ref[1, i] = jnp.where(wanted, jnp.maximum(row - device_row, 0) // block * batch + column, -1)

    copies = fill(zero_scr, back_ref, sems, early, back_ref.shape[0] // zero_scr.shape[0])
    for i in range(nowhere + 1):
        owner_scr[i] = -1
    for i in range(tall):
        column = scen * tall + i - tile * wide
        spot = jnp.where((column >= 0) & (column < wide), i * wide + column, nowhere)
        owner_scr[spot] = count + i
        spot_ref[count + i] = jnp.where(spot < nowhere, spot, -1)
    packed_scr[...] = jnp.zeros_like(packed_scr)
    diagonal = jnp.zeros((batch, block), jnp.float32)
    base = 0
    for piece in piece_refs:
        for i in range(piece.shape[0]):
            diagonal = diagonal + piece[i, half + 8:half + 8 + batch, :]
            for group in range(groups):
                label_scr[base + i, group] = piece[i, half, group].astype(jnp.int32)
        base += piece.shape[0]
    base = 0
    for piece in piece_refs:

        def add_one(i, unused, piece=piece, base=base):
            label = label_scr[base + i, 0]

            @pl.when((label >= 0) & (label < batch))
            def add():
                packed_scr[label] += piece[i, :half + 8, :]

            return unused

        lax.fori_loop(0, piece.shape[0], add_one, 0)
        base += piece.shape[0]
    row_id = lax.broadcasted_iota(jnp.int32, (block, block), 0)
    col_id = lax.broadcasted_iota(jnp.int32, (block, block), 1)
    for j in range(batch):
        values = unpack_upper(block, packed_scr[j, :half], packed_scr[j, half:half + 1])
        sum_scr[j * block:(j + 1) * block, :] = values + jnp.where(row_id == col_id, diagonal[j:j + 1, :], 0.0)
    lane = lax.broadcasted_iota(jnp.int32, (batch, block), 1)

    def eliminate(turn, unused):
        start = turn * PIVOTS
        rows = [sum_scr[pl.ds(start + a, batch, stride=block), :] for a in range(PIVOTS)]
        mults, pivots, done = pivot_rows(rows, start, lane)
        for a in range(PIVOTS):
            at = slice(a * batch, (a + 1) * batch)
            out_ref[pl.ds(start + a, batch, stride=block), :] = done[a]
            mult_scr[at, :] = mults[a]
            pivot_scr[at, :] = pivots[a]
        for n in range(per_turn):
            claim(turn * per_turn + n)
        pivot_lane = (col_id >= start) & (col_id < start + PIVOTS)
        for j in range(batch):
            high, middle, low = split_three(mult_scr[pl.ds(j, PIVOTS, stride=batch), :])
            left = jnp.concatenate([high, high, middle, high, middle, low])
            high, middle, low = split_three(pivot_scr[pl.ds(j, PIVOTS, stride=batch), :])
            right = jnp.concatenate([high, middle, high, low, middle, high])
            change = lax.dot_general(
                left.astype(jnp.bfloat16), right.astype(jnp.bfloat16),
                (((0,), (0,)), ((), ())), preferred_element_type=jnp.float32,
            )
            at = slice(j * block, (j + 1) * block)
            sum_scr[at, :] = jnp.where(pivot_lane, 0.0, sum_scr[at, :]) - change
        return unused

    lax.fori_loop(0, turns, eliminate, 0)
    for copy in copies:
        copy.wait()


def split(value):
    high = value.astype(jnp.bfloat16)
    low = (value - high.astype(jnp.float32)).astype(jnp.bfloat16)
    return high, low


def panel_kernel(batch, block, plan_ref, regular_ref, inverse_ref, *refs):
    *piece_refs, out_ref, sum_scr, out_scr, sems = refs
    share = out_ref.shape[0]
    tall = min(share, block)
    first_row = (lax.axis_index("scen") * lax.axis_size("tile") + lax.axis_index("tile")) * share
    sum_scr[...] = jnp.zeros_like(sum_scr)
    base = 0
    for piece in piece_refs:
        for i in range(piece.shape[0]):
            spot = plan_ref[1, base + i]

            @pl.when(spot >= 0)
            def add(piece=piece, i=i, spot=spot):
                at = pl.multiple_of(spot // batch * tall, tall)
                piece_at = pl.multiple_of(first_row % block // tall * tall, tall)
                sum_scr[spot % batch, pl.ds(at, tall), :] += piece[i, pl.ds(piece_at, tall), :]

        base += piece.shape[0]

    @pl.when(first_row < batch * block)
    def add_diagonal():
        for j in range(batch):
            row_id = first_row + lax.broadcasted_iota(jnp.int32, (share, block), 0)
            col_id = j * block + lax.broadcasted_iota(jnp.int32, (share, block), 1)
            sum_scr[j] += jnp.where(row_id == col_id, regular_ref[j:j + 1, :], 0.0)

    copies = []
    for j in range(batch):
        at = slice(j * block, (j + 1) * block)
        left = jnp.concatenate(split(sum_scr[j]), axis=1)
        high, low = split(inverse_ref[at, :])
        right = jnp.concatenate([
            jnp.concatenate([high, high], axis=1),
            jnp.concatenate([low, jnp.zeros_like(low)], axis=1),
        ])
        product = lax.dot_general(
            left, right, (((1,), (1,)), ((), ())), preferred_element_type=jnp.float32
        )
        out_scr[j] = product[:, :block] + product[:, block:]
        copies.append(pltpu.make_async_copy(out_scr.at[j], out_ref.at[:, at], sems.at[j]))
        copies[-1].start()
    for copy in copies:
        copy.wait()


def scatter_kernel(block, plan_ref, spot_ref, regular_ref, *refs):
    *piece_refs, back_ref, out_ref, sum_scr, sems = refs
    row_id = lax.broadcasted_iota(jnp.int32, (block, block), 0)
    col_id = lax.broadcasted_iota(jnp.int32, (block, block), 1)
    tall, wide = out_ref.shape[0] // block, out_ref.shape[1] // block
    count = sum(piece.shape[0] for piece in piece_refs)

    def diagonal_one(i, unused):
        @pl.when(spot_ref[count + i] >= 0)
        def put():
            sum_scr[count + i] = jnp.where(row_id == col_id, regular_ref[pl.ds(i, 1), :], 0.0)

        return unused

    lax.fori_loop(0, tall, diagonal_one, 0)
    base = 0
    for piece in piece_refs:

        def add_one(i, unused, piece=piece, base=base):
            owner = plan_ref[0, base + i]

            @pl.when(owner == base + i)
            def put():
                sum_scr[owner] = piece[i]

            @pl.when((owner >= 0) & (owner != base + i))
            def add():
                sum_scr[owner] += piece[i]

            return unused

        lax.fori_loop(0, piece.shape[0], add_one, 0)
        base += piece.shape[0]

    def copy(i):
        spot = spot_ref[i]
        row = pl.multiple_of(spot // wide * block, block)
        column = pl.multiple_of(spot % wide * block, block)
        return pltpu.make_async_copy(
            sum_scr.at[i], out_ref.at[pl.ds(row, block), pl.ds(column, block)], sems.at[i]
        )

    def start_one(i, unused):
        @pl.when(spot_ref[i] >= 0)
        def start():
            copy(i).start()

        return unused

    def wait_one(i, unused):
        @pl.when(spot_ref[i] >= 0)
        def wait():
            copy(i).wait()

        return unused

    lax.fori_loop(0, count + tall, start_one, 0)
    lax.fori_loop(0, count + tall, wait_one, 0)


def limit(*held):
    size = sum(math.prod(one.shape) * jnp.dtype(one.dtype).itemsize for one in held)
    return pltpu.CompilerParams(vmem_limit_bytes=min(size + 4 * MIB, 60 * MIB))


def local(inv_factor, border, touched, live_count, regular):
    scen_count = lax.axis_size("scen")
    tile_count = lax.axis_size("tile")
    scen_index = lax.axis_index("scen")
    tile_index = lax.axis_index("tile")
    local_count, order_size, width = border.shape
    groups = touched.shape[1]
    block = width // groups
    block_total = FIRST // block
    group_size = block_total // groups
    batch = PANEL // block
    ratio = scen_count // groups
    row_span = block_total // scen_count
    row_share = FIRST // (scen_count * tile_count)
    assert local_count == 1 and tile_count == groups and scen_count == groups * ratio
    assert batch <= group_size and batch * block <= regular.shape[0]
    corner_rows = block // 2 + 8 + batch
    both = ("scen", "tile")
    regular_rows = regular.reshape(-1, block)

    tall, wide = row_span * block, group_size * block
    early = int(tall // ZEROS * EARLY)
    zeros = [pltpu.VMEM((ZEROS, wide), jnp.float32), pltpu.SemaphoreType.DMA((tall // ZEROS,))]

    main, *first = pl.pallas_call(
        functools.partial(first_kernel, groups, block, group_size, ratio),
        in_specs=[SMEM, SMEM, VMEM, HBM, HBM],
        out_specs=[VMEM] * (groups + 1),
        out_shape=[jax.ShapeDtypeStruct((groups * groups, block, block), jnp.float32)]
        + [jax.ShapeDtypeStruct((corner_rows + block, block), jnp.float32)] * groups,
        scratch_shapes=[
            pltpu.VMEM((order_size, width), border.dtype),
            pltpu.VMEM((order_size, order_size), inv_factor.dtype),
            pltpu.VMEM((order_size, width), border.dtype),
            pltpu.VMEM((groups, block, block), jnp.float32),
            pltpu.SemaphoreType.DMA,
            pltpu.SemaphoreType.DMA((groups,)),
        ],
        compiler_params=pltpu.CompilerParams(vmem_limit_bytes=60 * MIB),
    )(touched, live_count, regular_rows, inv_factor[0], border[0])
    def along_place(array, k):
        pairs = [(s, (s // ratio ^ k) * ratio + s % ratio) for s in range(scen_count)]
        return lax.ppermute(array, "scen", pairs)

    def along_tile(array, k):
        return lax.ppermute(array, "tile", [(t, t ^ k) for t in range(tile_count)])

    def along_part(array, k):
        pairs = [(s, s // ratio * ratio + (s % ratio ^ k)) for s in range(scen_count)]
        return lax.ppermute(array, "scen", pairs)

    def along_tiles(array):
        return [array] + [along_tile(array, k) for k in range(1, tile_count)]

    def along_parts(pieces):
        return pieces + [along_part(piece, k) for k in range(1, ratio) for piece in pieces]

    firsts = [first[0]] + [along_place(first[k], k) for k in range(1, groups)]
    corners = along_tiles(jnp.stack([piece[:corner_rows] for piece in firsts]))
    background = pl.pallas_call(
        functools.partial(fill_kernel, early),
        in_specs=[ANY],
        out_specs=ANY,
        out_shape=jax.ShapeDtypeStruct((tall, wide), jnp.float32),
        scratch_shapes=zeros,
        cost_estimate=pl.CostEstimate(flops=0, bytes_accessed=4 * early * ZEROS * wide, transcendentals=0),
        compiler_params=limit(zeros[0]),
    )(corners[1])
    strip = jnp.stack([piece[corner_rows:] for piece in firsts])
    later, background = lax.optimization_barrier((strip, background))
    strips = [strip, along_tile(strip, 1)] + [along_tile(later, k) for k in range(2, tile_count)]
    corners = along_parts(corners)
    teams = [
        [(z * ratio + c) * tile_count + t for z in range(groups) for t in range(tile_count)]
        for c in range(ratio)
    ]
    blocks = lax.all_to_all(main, both, 0, 0, tiled=True, axis_index_groups=teams)
    count = scen_count * tile_count
    scratch = [
        pltpu.VMEM((batch, block // 2 + 8, block), jnp.float32),
        pltpu.VMEM((batch * block, block), jnp.float32),
        pltpu.VMEM((batch * PIVOTS, block), jnp.float32),
        pltpu.VMEM((batch * PIVOTS, block), jnp.float32),
        zeros[0],
    ]
    inverse, background, plan, spots = pl.pallas_call(
        functools.partial(factor_kernel, batch, block, ratio, row_share, early),
        in_specs=[VMEM] * len(corners) + [ANY],
        input_output_aliases={len(corners): 1},
        out_specs=[VMEM, ANY, SMEM, SMEM],
        out_shape=[
            jax.ShapeDtypeStruct((batch * block, block), jnp.float32),
            jax.ShapeDtypeStruct((tall, wide), jnp.float32),
            jax.ShapeDtypeStruct((2, count), jnp.int32),
            jax.ShapeDtypeStruct((count + row_span,), jnp.int32),
        ],
        scratch_shapes=scratch + [
            pltpu.SMEM((count, groups), jnp.int32),
            pltpu.SMEM((row_span * group_size + 1,), jnp.int32),
            zeros[1],
        ],
        compiler_params=limit(*corners, *scratch),
    )(*corners, background)

    strips, inverse = lax.optimization_barrier((strips, inverse))
    strips = along_parts(strips)
    blocks, inverse = lax.optimization_barrier((blocks, inverse))
    blocks = along_parts([blocks])

    total = pltpu.VMEM((count + row_span, block, block), jnp.float32)
    schur = pl.pallas_call(
        functools.partial(scatter_kernel, block),
        in_specs=[SMEM, SMEM, VMEM] + [VMEM] * len(blocks) + [ANY],
        out_specs=ANY,
        out_shape=jax.ShapeDtypeStruct((tall, wide), jnp.float32),
        input_output_aliases={3 + len(blocks): 0},
        scratch_shapes=[total, pltpu.SemaphoreType.DMA((count + row_span,))],
        compiler_params=limit(*blocks, total),
    )(plan, spots, regular_rows, *blocks, background)
    strips, schur = lax.optimization_barrier((strips, schur))
    sums = [pltpu.VMEM((batch, row_share, block), jnp.float32)] * 2
    panel = pl.pallas_call(
        functools.partial(panel_kernel, batch, block),
        in_specs=[SMEM, VMEM, VMEM] + [VMEM] * len(strips),
        out_specs=ANY,
        out_shape=jax.ShapeDtypeStruct((row_share, batch * block), jnp.float32),
        scratch_shapes=sums + [pltpu.SemaphoreType.DMA((batch,))],
        compiler_params=limit(*strips, *sums),
    )(plan, regular_rows, inverse, *strips)
    return (schur, panel)


def solution(mesh):
    return jax.shard_map(
        local,
        mesh=mesh,
        in_specs=(
            P(("scen", "tile"), None, None),
            P(("scen", "tile"), None, None),
            P(("scen", "tile"), None),
            P(("scen", "tile")),
            P("scen"),
        ),
        out_specs=(P("scen", "tile"), P(("scen", "tile"), None)),
        check_vma=False,
    )
```

```python
import functools
import math

import jax
import jax.numpy as jnp
from jax import lax
from jax.experimental import pallas as pl
from jax.experimental.pallas import tpu as pltpu
from jax.sharding import PartitionSpec as P

FIRST = 16384
PANEL = 1024
PIVOTS = 8
ZEROS = 64
EARLY = 0.25
MIB = 1 << 20

SMEM = pl.BlockSpec(memory_space=pltpu.SMEM)
VMEM = pl.BlockSpec(memory_space=pltpu.VMEM)
ANY = pl.BlockSpec(memory_space=pl.ANY)
HBM = pl.BlockSpec(memory_space=pltpu.HBM)


def gram(left, right):
    return lax.dot_general(left, right, (((0,), (0,)), ((), ())), preferred_element_type=jnp.float32)


def fill(zero_scr, back_ref, sems, first, last):
    tall = zero_scr.shape[0]
    zero_scr[...] = jnp.zeros_like(zero_scr)
    copies = [
        pltpu.make_async_copy(zero_scr, back_ref.at[i * tall:(i + 1) * tall], sems.at[i])
        for i in range(first, last)
    ]
    for copy in copies:
        copy.start()
    return copies


def first_kernel(
    groups, block, group_size, ratio, touched_ref, live_ref, regular_ref, inv_ref, border_ref,
    main_ref, *refs,
):
    *first_refs, scaled_ref, inv_scr, border_scr, column_scr, inv_sem, border_sems = refs
    place = lax.axis_index("scen") // ratio
    copies = []
    keeps, labels = [], []
    for group in range(groups):
        slot = jnp.int32(0)
        for m in range(groups):
            slot = jnp.where(touched_ref[0, m] // group_size == group, m, slot)
        copies.append(pltpu.make_async_copy(
            border_ref.at[:, pl.ds(pl.multiple_of(slot * block, block), block)],
            border_scr.at[:, group * block:(group + 1) * block],
            border_sems.at[group],
        ))
        keeps.append(slot < live_ref[0])
        labels.append(jnp.where(slot < live_ref[0], touched_ref[0, slot], -1).astype(jnp.float32))
    copies.append(pltpu.make_async_copy(inv_ref, inv_scr, inv_sem))
    for copy in copies:
        copy.start()
    keep = jnp.concatenate(
        [jnp.broadcast_to(keep.astype(jnp.float32), (1, block)) for keep in keeps], axis=1
    )
    for copy in copies:
        copy.wait()
    scaled = jnp.dot(inv_scr[...], border_scr[...], preferred_element_type=jnp.float32)
    scaled_ref[...] = jnp.where(keep > 0.0, scaled, 0.0).astype(scaled_ref.dtype)
    strip = gram(scaled_ref[:, :block], scaled_ref[...])
    half = block // 2
    corner_rows = first_refs[0].shape[0] - block
    corner = pack_corner(groups, strip[:, :block])
    is_root = (lax.axis_index("scen") == 0) & (lax.axis_index("tile") == 0)
    root_rows = regular_ref[:corner_rows - half - 8, :] * is_root.astype(jnp.float32)
    lane = lax.broadcasted_iota(jnp.int32, (8, block), 1)
    last = corner[half:]
    for group in range(groups):
        column_scr[group] = strip[:, group * block:(group + 1) * block].T
        last = jnp.where(lane == group, labels[group], last)
    for k in range(groups):
        first_refs[k][:half] = corner[:half]
        first_refs[k][half:half + 8] = last
        first_refs[k][half + 8:corner_rows] = root_rows
        first_refs[k][corner_rows:] = column_scr[place ^ k]
    for group in range(groups):
        if group > 0:
            strip = gram(scaled_ref[:, group * block:(group + 1) * block], scaled_ref[...])
        for other in range(groups):
            main_ref[group * groups + other] = strip[:, other * block:(other + 1) * block]


def fill_kernel(early, after_ref, back_ref, zero_scr, sems):
    for copy in fill(zero_scr, back_ref, sems, 0, early):
        copy.wait()


def pack_corner(groups, whole):
    block = whole.shape[0]
    half = block // 2
    assert groups <= half
    row_id = lax.broadcasted_iota(jnp.int32, (half, block), 0)
    col_id = lax.broadcasted_iota(jnp.int32, (half, block), 1)
    upper, lower = whole[:half], whole[half:]
    body = jnp.where(col_id >= row_id, upper, pltpu.roll(lower, half, 1))
    ends = jnp.sum(jnp.where(col_id == row_id + half, lower, 0.0), axis=0, keepdims=True)
    return jnp.concatenate([body, jnp.broadcast_to(ends, (8, block))])


def unpack_upper(block, packed, ends):
    half = block // 2
    row_id = lax.broadcasted_iota(jnp.int32, (half, block), 0)
    col_id = lax.broadcasted_iota(jnp.int32, (half, block), 1)
    low = jnp.where(col_id < row_id, packed, 0.0)
    turned = jnp.concatenate([low, jnp.zeros_like(low)]).T[:half]
    lower = pltpu.roll(turned, half, 1) + jnp.where(col_id == row_id + half, ends, 0.0)
    return jnp.concatenate([packed, lower])


def pivot_rows(rows, start, lane):
    count = len(rows)
    entry = {}
    for b in range(count):
        at = jnp.full(lane.shape, start + b, jnp.int32)
        for a in range(b + 1):
            entry[a, b] = jnp.take_along_axis(rows[a], at, axis=1, mode="promise_in_bounds")
    lower = {}
    for a in range(count):
        lower[a, a] = 1.0 / entry[a, a]
        for b in range(a + 1, count):
            lower[b, a] = entry[a, b] * lower[a, a]
            for c in range(b, count):
                entry[b, c] = entry[b, c] - lower[b, a] * entry[a, c]
    whole, mults, pivots, done = [], [], [], []
    for a in range(count):
        row = rows[a]
        for b in range(a):
            row = jnp.where(lane == start + b, 0.0, row) - lower[a, b] * whole[b]
        mults.append(jnp.where(lane >= start + count, row * lower[a, a], 0.0))
        whole.append(jnp.where(lane == start + a, 1.0, row))
        pivots.append(jnp.where((lane > start + a) & (lane < start + count), 0.0, whole[a]))
        done.append(jnp.where(lane <= start + a, whole[a] * lax.rsqrt(entry[a, a]), 0.0))
    return mults, pivots, done


def split_three(value):
    high = value.astype(jnp.bfloat16).astype(jnp.float32)
    rest = value - high
    middle = rest.astype(jnp.bfloat16).astype(jnp.float32)
    return high, middle, rest - middle


def factor_kernel(batch, block, ratio, share, early, *refs):
    (*piece_refs, in_ref, out_ref, back_ref, plan_ref, spot_ref,
     packed_scr, sum_scr, mult_scr, pivot_scr, zero_scr, label_scr, owner_scr, sems) = refs
    half = block // 2
    scen, tile = lax.axis_index("scen"), lax.axis_index("tile")
    tile_count = lax.axis_size("tile")
    place = scen // ratio
    tall, wide = back_ref.shape[0] // block, back_ref.shape[1] // block
    count, groups = label_scr.shape
    turns = block // PIVOTS
    per_turn = -(-count // turns)
    assert count % turns == 0
    nowhere = tall * wide
    device_row = (scen * tile_count + tile) * share

    def claim(i):
        part, sent = i // (tile_count * groups), i % (tile_count * groups)
        sender = part * (tile_count * groups) + ((sent % tile_count) ^ tile) * groups + ((sent // tile_count) ^ place)
        row, column = label_scr[sender, place], label_scr[sender, tile]
        inside = (row >= scen * tall) & (row < (scen + 1) * tall) & (column >= 0)
        spot = jnp.where(inside, (row - scen * tall) * wide + column - tile * wide, nowhere)
        owner = owner_scr[spot]
        owner = jnp.where(inside, jnp.where(owner < 0, i, owner), -1)
        owner_scr[spot] = owner
        plan_ref[0, i] = owner
        spot_ref[i] = jnp.where(owner == i, spot, -1)
        row, column = label_scr[i, place] * block, label_scr[i, 0]
        wanted = (column >= 0) & (column < batch) & (row >= 0)
        wanted = wanted & (row < device_row + share) & (device_row < row + block)
        plan_ref[1, i] = jnp.where(wanted, jnp.maximum(row - device_row, 0) // block * batch + column, -1)

    copies = fill(zero_scr, back_ref, sems, early, back_ref.shape[0] // zero_scr.shape[0])
    for i in range(nowhere + 1):
        owner_scr[i] = -1
    for i in range(tall):
        column = scen * tall + i - tile * wide
        spot = jnp.where((column >= 0) & (column < wide), i * wide + column, nowhere)
        owner_scr[spot] = count + i
        spot_ref[count + i] = jnp.where(spot < nowhere, spot, -1)
    packed_scr[...] = jnp.zeros_like(packed_scr)
    diagonal = jnp.zeros((batch, block), jnp.float32)
    base = 0
    for piece in piece_refs:
        for i in range(piece.shape[0]):
            diagonal = diagonal + piece[i, half + 8:half + 8 + batch, :]
            for group in range(groups):
                label_scr[base + i, group] = piece[i, half, group].astype(jnp.int32)
        base += piece.shape[0]
    base = 0
    for piece in piece_refs:

        def add_one(i, unused, piece=piece, base=base):
            label = label_scr[base + i, 0]

            @pl.when((label >= 0) & (label < batch))
            def add():
                packed_scr[label] += piece[i, :half + 8, :]

            return unused

        lax.fori_loop(0, piece.shape[0], add_one, 0)
        base += piece.shape[0]
    row_id = lax.broadcasted_iota(jnp.int32, (block, block), 0)
    col_id = lax.broadcasted_iota(jnp.int32, (block, block), 1)
    for j in range(batch):
        values = unpack_upper(block, packed_scr[j, :half], packed_scr[j, half:half + 1])
        sum_scr[j * block:(j + 1) * block, :] = values + jnp.where(row_id == col_id, diagonal[j:j + 1, :], 0.0)
    lane = lax.broadcasted_iota(jnp.int32, (batch, block), 1)

    def eliminate(turn, unused):
        start = turn * PIVOTS
        rows = [sum_scr[pl.ds(start + a, batch, stride=block), :] for a in range(PIVOTS)]
        mults, pivots, done = pivot_rows(rows, start, lane)
        for a in range(PIVOTS):
            at = slice(a * batch, (a + 1) * batch)
            out_ref[pl.ds(start + a, batch, stride=block), :] = done[a]
            mult_scr[at, :] = mults[a]
            pivot_scr[at, :] = pivots[a]
        for n in range(per_turn):
            claim(turn * per_turn + n)
        pivot_lane = (col_id >= start) & (col_id < start + PIVOTS)
        for j in range(batch):
            high, middle, low = split_three(mult_scr[pl.ds(j, PIVOTS, stride=batch), :])
            left = jnp.concatenate([high, high, middle, high, middle, low])
            high, middle, low = split_three(pivot_scr[pl.ds(j, PIVOTS, stride=batch), :])
            right = jnp.concatenate([high, middle, high, low, middle, high])
            change = lax.dot_general(
                left.astype(jnp.bfloat16), right.astype(jnp.bfloat16),
                (((0,), (0,)), ((), ())), preferred_element_type=jnp.float32,
            )
            at = slice(j * block, (j + 1) * block)
            sum_scr[at, :] = jnp.where(pivot_lane, 0.0, sum_scr[at, :]) - change
        return unused

    lax.fori_loop(0, turns, eliminate, 0)
    for copy in copies:
        copy.wait()


def split(value):
    high = value.astype(jnp.bfloat16)
    low = (value - high.astype(jnp.float32)).astype(jnp.bfloat16)
    return high, low


def panel_kernel(batch, block, plan_ref, regular_ref, inverse_ref, *refs):
    *piece_refs, out_ref, sum_scr, out_scr, sems = refs
    share = out_ref.shape[0]
    tall = min(share, block)
    first_row = (lax.axis_index("scen") * lax.axis_size("tile") + lax.axis_index("tile")) * share
    sum_scr[...] = jnp.zeros_like(sum_scr)
    base = 0
    for piece in piece_refs:
        for i in range(piece.shape[0]):
            spot = plan_ref[1, base + i]

            @pl.when(spot >= 0)
            def add(piece=piece, i=i, spot=spot):
                at = pl.multiple_of(spot // batch * tall, tall)
                piece_at = pl.multiple_of(first_row % block // tall * tall, tall)
                sum_scr[spot % batch, pl.ds(at, tall), :] += piece[i, pl.ds(piece_at, tall), :]

        base += piece.shape[0]

    @pl.when(first_row < batch * block)
    def add_diagonal():
        for j in range(batch):
            row_id = first_row + lax.broadcasted_iota(jnp.int32, (share, block), 0)
            col_id = j * block + lax.broadcasted_iota(jnp.int32, (share, block), 1)
            sum_scr[j] += jnp.where(row_id == col_id, regular_ref[j:j + 1, :], 0.0)

    copies = []
    for j in range(batch):
        at = slice(j * block, (j + 1) * block)
        left = jnp.concatenate(split(sum_scr[j]), axis=1)
        high, low = split(inverse_ref[at, :])
        right = jnp.concatenate([
            jnp.concatenate([high, high], axis=1),
            jnp.concatenate([low, jnp.zeros_like(low)], axis=1),
        ])
        product = lax.dot_general(
            left, right, (((1,), (1,)), ((), ())), preferred_element_type=jnp.float32
        )
        out_scr[j] = product[:, :block] + product[:, block:]
        copies.append(pltpu.make_async_copy(out_scr.at[j], out_ref.at[:, at], sems.at[j]))
        copies[-1].start()
    for copy in copies:
        copy.wait()


def scatter_kernel(block, plan_ref, spot_ref, regular_ref, *refs):
    *piece_refs, back_ref, out_ref, sum_scr, sems = refs
    row_id = lax.broadcasted_iota(jnp.int32, (block, block), 0)
    col_id = lax.broadcasted_iota(jnp.int32, (block, block), 1)
    tall, wide = out_ref.shape[0] // block, out_ref.shape[1] // block
    count = sum(piece.shape[0] for piece in piece_refs)

    def diagonal_one(i, unused):
        @pl.when(spot_ref[count + i] >= 0)
        def put():
            sum_scr[count + i] = jnp.where(row_id == col_id, regular_ref[pl.ds(i, 1), :], 0.0)

        return unused

    lax.fori_loop(0, tall, diagonal_one, 0)
    base = 0
    for piece in piece_refs:

        def add_one(i, unused, piece=piece, base=base):
            owner = plan_ref[0, base + i]

            @pl.when(owner == base + i)
            def put():
                sum_scr[owner] = piece[i]

            @pl.when((owner >= 0) & (owner != base + i))
            def add():
                sum_scr[owner] += piece[i]

            return unused

        lax.fori_loop(0, piece.shape[0], add_one, 0)
        base += piece.shape[0]

    def copy(i):
        spot = spot_ref[i]
        row = pl.multiple_of(spot // wide * block, block)
        column = pl.multiple_of(spot % wide * block, block)
        return pltpu.make_async_copy(
            sum_scr.at[i], out_ref.at[pl.ds(row, block), pl.ds(column, block)], sems.at[i]
        )

    def start_one(i, unused):
        @pl.when(spot_ref[i] >= 0)
        def start():
            copy(i).start()

        return unused

    def wait_one(i, unused):
        @pl.when(spot_ref[i] >= 0)
        def wait():
            copy(i).wait()

        return unused

    lax.fori_loop(0, count + tall, start_one, 0)
    lax.fori_loop(0, count + tall, wait_one, 0)


def limit(*held):
    size = sum(math.prod(one.shape) * jnp.dtype(one.dtype).itemsize for one in held)
    return pltpu.CompilerParams(vmem_limit_bytes=min(size + 4 * MIB, 60 * MIB))


def local(inv_factor, border, touched, live_count, regular):
    scen_count = lax.axis_size("scen")
    tile_count = lax.axis_size("tile")
    scen_index = lax.axis_index("scen")
    tile_index = lax.axis_index("tile")
    local_count, order_size, width = border.shape
    groups = touched.shape[1]
    block = width // groups
    block_total = FIRST // block
    group_size = block_total // groups
    batch = PANEL // block
    ratio = scen_count // groups
    row_span = block_total // scen_count
    row_share = FIRST // (scen_count * tile_count)
    assert local_count == 1 and tile_count == groups and scen_count == groups * ratio
    assert batch <= group_size and batch * block <= regular.shape[0]
    corner_rows = block // 2 + 8 + batch
    both = ("scen", "tile")
    regular_rows = regular.reshape(-1, block)

    tall, wide = row_span * block, group_size * block
    early = int(tall // ZEROS * EARLY)
    zeros = [pltpu.VMEM((ZEROS, wide), jnp.float32), pltpu.SemaphoreType.DMA((tall // ZEROS,))]

    main, *first = pl.pallas_call(
        functools.partial(first_kernel, groups, block, group_size, ratio),
        in_specs=[SMEM, SMEM, VMEM, HBM, HBM],
        out_specs=[VMEM] * (groups + 1),
        out_shape=[jax.ShapeDtypeStruct((groups * groups, block, block), jnp.float32)]
        + [jax.ShapeDtypeStruct((corner_rows + block, block), jnp.float32)] * groups,
        scratch_shapes=[
            pltpu.VMEM((order_size, width), border.dtype),
            pltpu.VMEM((order_size, order_size), inv_factor.dtype),
            pltpu.VMEM((order_size, width), border.dtype),
            pltpu.VMEM((groups, block, block), jnp.float32),
            pltpu.SemaphoreType.DMA,
            pltpu.SemaphoreType.DMA((groups,)),
        ],
        compiler_params=pltpu.CompilerParams(vmem_limit_bytes=60 * MIB),
    )(touched, live_count, regular_rows, inv_factor[0], border[0])
    def along_place(array, k):
        pairs = [(s, (s // ratio ^ k) * ratio + s % ratio) for s in range(scen_count)]
        return lax.ppermute(array, "scen", pairs)

    def along_tile(array, k):
        return lax.ppermute(array, "tile", [(t, t ^ k) for t in range(tile_count)])

    def along_part(array, k):
        pairs = [(s, s // ratio * ratio + (s % ratio ^ k)) for s in range(scen_count)]
        return lax.ppermute(array, "scen", pairs)

    def along_tiles(array):
        return [array] + [along_tile(array, k) for k in range(1, tile_count)]

    def along_parts(pieces):
        return pieces + [along_part(piece, k) for k in range(1, ratio) for piece in pieces]

    firsts = [first[0]] + [along_place(first[k], k) for k in range(1, groups)]
    corners = along_tiles(jnp.stack([piece[:corner_rows] for piece in firsts]))
    background = pl.pallas_call(
        functools.partial(fill_kernel, early),
        in_specs=[ANY],
        out_specs=ANY,
        out_shape=jax.ShapeDtypeStruct((tall, wide), jnp.float32),
        scratch_shapes=zeros,
        cost_estimate=pl.CostEstimate(flops=0, bytes_accessed=4 * early * ZEROS * wide, transcendentals=0),
        compiler_params=limit(zeros[0]),
    )(corners[1])
    strip = jnp.stack([piece[corner_rows:] for piece in firsts])
    later, background = lax.optimization_barrier((strip, background))
    strips = [strip, along_tile(strip, 1)] + [along_tile(later, k) for k in range(2, tile_count)]
    corners = along_parts(corners)
    teams = [
        [(z * ratio + c) * tile_count + t for z in range(groups) for t in range(tile_count)]
        for c in range(ratio)
    ]
    blocks = lax.all_to_all(main, both, 0, 0, tiled=True, axis_index_groups=teams)
    count = scen_count * tile_count
    scratch = [
        pltpu.VMEM((batch, block // 2 + 8, block), jnp.float32),
        pltpu.VMEM((batch * block, block), jnp.float32),
        pltpu.VMEM((batch * PIVOTS, block), jnp.float32),
        pltpu.VMEM((batch * PIVOTS, block), jnp.float32),
        zeros[0],
    ]
    inverse, background, plan, spots = pl.pallas_call(
        functools.partial(factor_kernel, batch, block, ratio, row_share, early),
        in_specs=[VMEM] * len(corners) + [ANY],
        input_output_aliases={len(corners): 1},
        out_specs=[VMEM, ANY, SMEM, SMEM],
        out_shape=[
            jax.ShapeDtypeStruct((batch * block, block), jnp.float32),
            jax.ShapeDtypeStruct((tall, wide), jnp.float32),
            jax.ShapeDtypeStruct((2, count), jnp.int32),
            jax.ShapeDtypeStruct((count + row_span,), jnp.int32),
        ],
        scratch_shapes=scratch + [
            pltpu.SMEM((count, groups), jnp.int32),
            pltpu.SMEM((row_span * group_size + 1,), jnp.int32),
            zeros[1],
        ],
        compiler_params=limit(*corners, *scratch),
    )(*corners, background)

    strips, inverse = lax.optimization_barrier((strips, inverse))
    strips = along_parts(strips)
    blocks, inverse = lax.optimization_barrier((blocks, inverse))
    blocks = along_parts([blocks])

    total = pltpu.VMEM((count + row_span, block, block), jnp.float32)
    schur = pl.pallas_call(
        functools.partial(scatter_kernel, block),
        in_specs=[SMEM, SMEM, VMEM] + [VMEM] * len(blocks) + [ANY],
        out_specs=ANY,
        out_shape=jax.ShapeDtypeStruct((tall, wide), jnp.float32),
        input_output_aliases={3 + len(blocks): 0},
        scratch_shapes=[total, pltpu.SemaphoreType.DMA((count + row_span,))],
        compiler_params=limit(*blocks, total),
    )(plan, spots, regular_rows, *blocks, background)
    strips, schur = lax.optimization_barrier((strips, schur))
    sums = [pltpu.VMEM((batch, row_share, block), jnp.float32)] * 2
    panel = pl.pallas_call(
        functools.partial(panel_kernel, batch, block),
        in_specs=[SMEM, VMEM, VMEM] + [VMEM] * len(strips),
        out_specs=ANY,
        out_shape=jax.ShapeDtypeStruct((row_share, batch * block), jnp.float32),
        scratch_shapes=sums + [pltpu.SemaphoreType.DMA((batch,))],
        compiler_params=limit(*strips, *sums),
    )(plan, regular_rows, inverse, *strips)
    return (schur, panel)


def solution(mesh):
    return jax.shard_map(
        local,
        mesh=mesh,
        in_specs=(
            P(("scen", "tile"), None, None),
            P(("scen", "tile"), None, None),
            P(("scen", "tile"), None),
            P(("scen", "tile")),
            P("scen"),
        ),
        out_specs=(P("scen", "tile"), P(("scen", "tile"), None)),
        check_vma=False,
    )
```
